768 devices in a mesh: dp: 48 (over x, z), fsdp: 16 (over y, core).
Axes of the slice: x: 4, y: 8, z: 12, core: 2. Of those that a mesh axis runs over, the one named last changes fastest.
Arguments:
- train_x: bfloat16 [12288, 4096], P('dp', 'fsdp'), may hold values from -0.75 to 0.75
- train_attn: bfloat16 [12288, 4096], P('dp', 'fsdp'), may hold values from -0.75 to 0.75
- train_gqkv: bfloat16 [12288, 6144], P('dp', 'fsdp'), may hold values from -0.65625 to 0.65625
- train_go: bfloat16 [12288, 4096], P('dp', 'fsdp'), may hold values from -0.65625 to 0.65625
- train_lengths: int32 [48, 4], P('dp'), may hold values from 1 to 128, 256 in all within a row
- val_x: bfloat16 [48, 32, 4096], P('dp', None, 'fsdp'), may hold values from -0.75 to 0.75
- val_attn: bfloat16 [48, 32, 4096], P('dp', None, 'fsdp'), may hold values from -0.75 to 0.75
- val_gqkv: bfloat16 [48, 32, 6144], P('dp', None, 'fsdp'), may hold values from -0.65625 to 0.65625
- val_go: bfloat16 [48, 32, 4096], P('dp', None, 'fsdp'), may hold values from -0.65625 to 0.65625
- val_lengths: int32 [48], replicated, may hold values from 1 to 32, 1152 in all
Outputs:
- scores: float32 [192, 48], P('dp', 'fsdp')
The draws below stay inside these ranges and needn't reach their ends.
Inputs may be any that keep to these rules, and one draw needn't show every extreme that they name: `train_lengths`: each row sums to 256; its sequences fill that index's token rows in order; the longest of all is 128. `val_lengths`: the valid positions of a sequence are its first ones; all sum to 1152; the longest is 32.
All inputs are finite; a program needn't handle non-finite values.
Results may differ from the reference program's by a relative error of at most 0.0003.
Values may be sent and summed in bfloat16 or wider, within the bound.
No kernel may reach another device: no remote copies, remote signals or barrier semaphores. Data moves between devices by JAX's collectives and lax.ppermute only.
A program may use at most 32 MiB of HBM per device.

```python
import math
import jax
import jax.numpy as jnp
import numpy as np
from jax import lax

D = 4096
TOK_DEV = 256
SEQ_DEV = 4
VLEN = 32
QKV = 6144
DP_GROUPS = 48
TOKENS = 12288
TRAIN_SEQ = 192
VAL_SEQ = 48


def level_of(stream_key, dims, shards, smallest, top_value):
    level = 1.0
    for axis_at, shards_of in shards:
        steps = jax.random.uniform(jax.random.fold_in(jax.random.fold_in(stream_key, 6), axis_at), (shards_of,), jnp.float32, smallest / len(shards), top_value / len(shards))
        level = level * jnp.repeat(jnp.exp(steps), dims[axis_at] // shards_of).reshape((-1,) + (1,) * (len(dims) - 1 - axis_at))
    return level


def length_profile(count, total, bound, slope):
    loads = [(1 << 20) // math.isqrt(grade ** slope) + 1 for grade in range(2, count + 1)]
    spare, counts = total - bound - (count - 1), [1] * (count - 1)
    while spare > 0:
        free = [i for i in range(count - 1) if counts[i] < bound]
        pool, budget = sum([loads[i] for i in free]), spare
        for i in free:
            addition = min(bound - counts[i], max(1, budget * loads[i] // pool), spare)
            counts[i] = counts[i] + addition
            spare = spare - addition
    return np.array([bound] + counts)


def ragged_sizes(own_key, number_of, total, most, skew):
    if number_of == 2:
        one = jax.random.randint(own_key, (), max(1, total - most), min(most, total - 1) + 1)
        return jnp.stack([one, total - one])
    lengths = jnp.asarray(length_profile(number_of, total, most, skew), jnp.int32)
    pairs = (number_of - 1) // 2
    source_of, sink = lengths[1:1 + 2 * pairs:2], lengths[2:2 + 2 * pairs:2]
    margin = jnp.minimum(source_of - 1, most - sink)
    moved = jax.random.randint(jax.random.fold_in(own_key, 1), (pairs,), 0, 1 << 20) % (margin + 1)
    lengths = lengths.at[1:1 + 2 * pairs:2].set(source_of - moved).at[2:2 + 2 * pairs:2].set(sink + moved)
    return lengths[jax.random.permutation(jax.random.fold_in(own_key, 2), number_of)]


def normal_values(key, dims, spread, bound, shards=(), kind=jnp.bfloat16):
    result = spread * jax.random.normal(key, dims, jnp.float32)
    if shards:
        result = result * level_of(key, dims, shards, -0.22, 0.18)
    return jnp.clip(result, -bound, bound).astype(kind)


def setup_inputs(seed: int = 0) -> dict:
    keys = jax.random.split(jax.random.key(seed), 11)
    return {
        "train_x": normal_values(keys[0], (TOKENS, D), 0.125, 0.75, ((0, 48), (1, 16))),
        "train_attn": normal_values(keys[1], (TOKENS, D), 0.125, 0.75, ((0, 48), (1, 16))),
        "train_gqkv": normal_values(keys[2], (TOKENS, QKV), 0.11, 0.65625, ((0, 48), (1, 16))),
        "train_go": normal_values(keys[3], (TOKENS, D), 0.11, 0.65625, ((0, 48), (1, 16))),
        "train_lengths": jax.vmap(lambda own: ragged_sizes(own, SEQ_DEV, TOK_DEV, TOK_DEV // 2, 2))(jax.random.split(keys[4], DP_GROUPS)).reshape((DP_GROUPS, SEQ_DEV)).astype(jnp.int32),
        "val_x": normal_values(keys[5], (VAL_SEQ, VLEN, D), 0.125, 0.75, ((0, 48), (2, 16))),
        "val_attn": normal_values(keys[6], (VAL_SEQ, VLEN, D), 0.125, 0.75, ((0, 48), (2, 16))),
        "val_gqkv": normal_values(keys[7], (VAL_SEQ, VLEN, QKV), 0.11, 0.65625, ((0, 48), (2, 16))),
        "val_go": normal_values(keys[8], (VAL_SEQ, VLEN, D), 0.11, 0.65625, ((0, 48), (2, 16))),
        "val_lengths": ragged_sizes(keys[9], VAL_SEQ, VAL_SEQ * VLEN * 3 // 4, VLEN, 2).astype(jnp.int32),
    }


score_scale = 0.015625


def reference(train_x, train_attn, train_gqkv, train_go, train_lengths, val_x, val_attn, val_gqkv, val_go, val_lengths):
    highest = lax.Precision.HIGHEST
    places = jnp.arange(VLEN, dtype=jnp.int32)
    val_mask = (places[None, :] < val_lengths[:, None]).astype(jnp.float32)
    wide_x = val_x.astype(jnp.float32)
    wide_attn = val_attn.astype(jnp.float32)
    wide_q = val_gqkv.astype(jnp.float32)
    wide_o = val_go.astype(jnp.float32)

    def block_scores(group_index):
        offset = (group_index * TOK_DEV).astype(jnp.int32)
        rows_x = lax.dynamic_slice_in_dim(train_x, offset, TOK_DEV, 0).astype(jnp.float32)
        rows_attn = lax.dynamic_slice_in_dim(train_attn, offset, TOK_DEV, 0).astype(jnp.float32)
        rows_q = lax.dynamic_slice_in_dim(train_gqkv, offset, TOK_DEV, 0).astype(jnp.float32)
        rows_o = lax.dynamic_slice_in_dim(train_go, offset, TOK_DEV, 0).astype(jnp.float32)
        lengths_row = lax.dynamic_index_in_dim(train_lengths, group_index, 0, keepdims=False)
        gram_x = jnp.einsum("td,mnd->mnt", rows_x, wide_x, precision=highest)
        gram_attn = jnp.einsum("td,mnd->mnt", rows_attn, wide_attn, precision=highest)
        gram_q = jnp.einsum("tc,mnc->mnt", rows_q, wide_q, precision=highest)
        gram_o = jnp.einsum("tc,mnc->mnt", rows_o, wide_o, precision=highest)
        contrib = gram_x * gram_q + gram_attn * gram_o
        per_token = jnp.sum(contrib * val_mask[:, :, None], axis=1)
        seq_ends = jnp.cumsum(lengths_row)
        seq_starts = seq_ends - lengths_row
        token_places = jnp.arange(TOK_DEV, dtype=jnp.int32)[:, None]
        members = ((token_places >= seq_starts[None, :]) & (token_places < seq_ends[None, :])).astype(jnp.float32)
        return jnp.dot(members.T, per_token.T, precision=highest)

    blocks = lax.map(block_scores, jnp.arange(DP_GROUPS, dtype=jnp.int32))
    return blocks.reshape(TRAIN_SEQ, VAL_SEQ) * score_scale
```

```python
import numpy as np
import jax
import jax.numpy as jnp
from jax import lax
from jax.experimental import pallas as pl
from jax.experimental.pallas import tpu as pltpu
from jax.sharding import Mesh, PartitionSpec as P

score_scale = 0.015625

NX, NZ, NY, NC = 4, 12, 8, 2
TOK, VLEN = 256, 32
SEQS = 6
ROWS = SEQS * VLEN
HALF = ROWS // 2
COLS = ((0, 256), (256, 512), (512, 896), (896, 1152))
WIDTH = 1152

SWAP = [
    ((6 * a + r) * NY + b, (6 * b + r) * NY + a)
    for a in range(NY)
    for b in range(NY)
    for r in range(SEQS)
]


def around(size, shift):
    return [(i, (i + shift) % size) for i in range(size)]


def gram_kernel(train, own, right, left, far, out, tbuf, vbuf, sems):
    x = lax.axis_index("x")
    copies = [pltpu.make_async_copy(train, tbuf, sems.at[0])]
    for k, (ref, shift) in enumerate(((own, 0), (right, 1), (left, 3), (far, 2))):
        at = lax.rem(x + shift, NX)
        copies.append(pltpu.make_async_copy(ref, vbuf.at[at], sems.at[k + 1]))
    for c in copies:
        c.start()
    for c in copies:
        c.wait()
    for g, (lo, hi) in enumerate(COLS):
        acc = jnp.zeros((ROWS, TOK), jnp.float32)
        for b in range(NY):
            v = vbuf[b // 2, (b % 2) * ROWS : (b % 2 + 1) * ROWS, lo:hi]
            t = tbuf[b, :, lo:hi]
            acc += lax.dot_general(
                v, t, (((1,), (1,)), ((), ())), preferred_element_type=jnp.float32
            )
        out[0, g] = acc[:HALF]
        out[1, g] = acc[HALF:]


def grams(train, own, right, left, far):
    any_spec = pl.BlockSpec(memory_space=pl.ANY)
    return pl.pallas_call(
        gram_kernel,
        out_shape=jax.ShapeDtypeStruct((2, 4, HALF, TOK), jnp.float32),
        in_specs=[any_spec] * 5,
        out_specs=pl.BlockSpec(memory_space=pltpu.VMEM),
        scratch_shapes=[
            pltpu.VMEM((NY, TOK, WIDTH), jnp.bfloat16),
            pltpu.VMEM((NX, 2 * ROWS, WIDTH), jnp.bfloat16),
            pltpu.SemaphoreType.DMA((5,)),
        ],
        compiler_params=pltpu.CompilerParams(vmem_limit_bytes=32 * 1024 * 1024),
    )(train, own, right, left, far)


def score_kernel(tl, vl, mine, other, out):
    first = 3 * (2 * lax.axis_index("y") + lax.axis_index("core"))
    g = mine[...] + other[...]
    contrib = g[0] * g[2] + g[1] * g[3]
    places = lax.broadcasted_iota(jnp.int32, (VLEN, TOK), 0)
    tokens = lax.broadcasted_iota(jnp.int32, (1, TOK), 1)
    rows = lax.broadcasted_iota(jnp.int32, (4, 3), 0)
    cols = lax.broadcasted_iota(jnp.int32, (4, 3), 1)
    result = jnp.zeros((4, 3), jnp.float32)
    for s in range(3):
        block = contrib[s * VLEN : (s + 1) * VLEN]
        per_token = jnp.sum(
            jnp.where(places < vl[first + s], block, 0.0), axis=0, keepdims=True
        )
        start = jnp.int32(0)
        for k in range(4):
            end = start + tl[0, k]
            inside = (tokens >= start) & (tokens < end)
            total = jnp.sum(
                jnp.where(inside, per_token, 0.0), axis=1, keepdims=True
            )
            result = jnp.where((rows == k) & (cols == s), total, result)
            start = end
    out[...] = result * score_scale


def scores_of(tl, vl, mine, other):
    smem = pl.BlockSpec(memory_space=pltpu.SMEM)
    vmem = pl.BlockSpec(memory_space=pltpu.VMEM)
    return pl.pallas_call(
        score_kernel,
        out_shape=jax.ShapeDtypeStruct((4, 3), jnp.float32),
        in_specs=[smem, smem, vmem, vmem],
        out_specs=vmem,
    )(tl, vl, mine, other)


def local(tx, ta, tq, to, tl, vx, va, vq, vo, vl):
    val = jnp.concatenate((vx[0], va[0], vq[0], vo[0]), axis=1)
    train = jnp.concatenate((tx, ta, tq, to), axis=1)
    val = lax.ppermute(val, ("x", "z", "y"), SWAP)
    full = lax.all_gather(train, "y", axis=0, tiled=False)
    own = lax.all_gather(val, "z", axis=0, tiled=True)
    left = lax.ppermute(own, "x", around(NX, 1))
    right = lax.ppermute(own, "x", around(NX, -1))
    far = jnp.concatenate(
        (
            lax.ppermute(left[:ROWS], "x", around(NX, 1)),
            lax.ppermute(right[ROWS:], "x", around(NX, -1)),
        )
    )
    both = grams(full, own, right, left, far)
    c = lax.axis_index("core")
    mine = lax.dynamic_index_in_dim(both, c, 0, keepdims=False)
    send = lax.dynamic_index_in_dim(both, 1 - c, 0, keepdims=False)
    other = lax.ppermute(send, "core", [(0, 1), (1, 0)])
    return scores_of(tl, vl, mine, other)


def solution(mesh):
    fine = Mesh(mesh.devices.reshape(NX, NZ, NY, NC), ("x", "z", "y", "core"))
    dp, fsdp = ("x", "z"), ("y", "core")
    in_specs = (
        (P(dp, fsdp),) * 4 + (P(dp, None),) + (P(dp, None, fsdp),) * 4 + (P(),)
    )
    return jax.shard_map(
        local, mesh=fine, in_specs=in_specs, out_specs=P(dp, fsdp), check_vma=False
    )
```

```python
import numpy as np
import jax
import jax.numpy as jnp
from jax import lax
from jax.experimental import pallas as pl
from jax.experimental.pallas import tpu as pltpu
from jax.sharding import Mesh, PartitionSpec as P

score_scale = 0.015625

NX, NZ, NY, NC = 4, 12, 8, 2
TOK, VLEN = 256, 32
SEQS = 6
ROWS = SEQS * VLEN
HALF = ROWS // 2
COLS = ((0, 256), (256, 512), (512, 896), (896, 1152))
WIDTH = 1152

def deal(shift):
    pairs = []
    for a in range(NY):
        for s in range(NX * NZ):
            x, z = divmod(s, NZ)
            to = x * NZ + (z - shift) % NZ
            pairs.append(((SEQS * a + s % SEQS) * NY + s // SEQS, to * NY + a))
    return pairs


def around(size, shift):
    return [(i, (i + shift) % size) for i in range(size)]


def gram_kernel(*refs):
    trains, vals = refs[:NY], refs[NY : NY + 3]
    mine, send, tbuf, vbuf, tsem, vsem = refs[NY + 3 :]
    x, z = lax.axis_index("x"), lax.axis_index("z")
    y, core = lax.axis_index("y"), lax.axis_index("core")
    vcopy = [pltpu.make_async_copy(r, vbuf.at[i], vsem.at[i]) for i, r in enumerate(vals)]
    tcopy = [pltpu.make_async_copy(r, tbuf.at[i], tsem.at[i]) for i, r in enumerate(trains)]
    for c in vcopy + tcopy:
        c.start()
    for c in vcopy:
        c.wait()
    for k in range(NY):
        tcopy[k].wait()
        b = lax.rem(y + k, NY)
        for half, out in ((1 - core, send), (core, mine)):
            blocks = []
            for r in range(3):
                s = SEQS * b + 3 * half + r
                dx = lax.rem(s // NZ - x + NX, NX)
                dz = lax.rem(lax.rem(s, NZ) - z + NZ, NZ)
                kind = lax.rem(dz, 3)
                step = jnp.where(kind == 2, lax.rem((dz + 1) // 3, 4), dz // 3)
                blocks.append((kind, dx * 4 + step))
            for g, (lo, hi) in enumerate(COLS):
                v = jnp.concatenate([vbuf[p, q, :, lo:hi] for p, q in blocks])
                d = lax.dot_general(
                    v,
                    tbuf[k, :, lo:hi],
                    (((1,), (1,)), ((), ())),
                    preferred_element_type=jnp.float32,
                )
                if k == 0:
                    out[g] = d
                else:
                    out[g] += d


def grams(trains, vals):
    half = jax.ShapeDtypeStruct((4, HALF, TOK), jnp.float32)
    vmem = pl.BlockSpec(memory_space=pltpu.VMEM)
    return pl.pallas_call(
        gram_kernel,
        out_shape=(half, half),
        in_specs=[pl.BlockSpec(memory_space=pl.ANY)] * (NY + 3),
        out_specs=(vmem, vmem),
        scratch_shapes=[
            pltpu.VMEM((NY, TOK, WIDTH), jnp.bfloat16),
            pltpu.VMEM((3, 16, VLEN, WIDTH), jnp.bfloat16),
            pltpu.SemaphoreType.DMA((NY,)),
            pltpu.SemaphoreType.DMA((3,)),
        ],
        compiler_params=pltpu.CompilerParams(vmem_limit_bytes=32 * 1024 * 1024),
    )(*trains, *vals)


def score_kernel(tl, vl, mine_any, other_any, out, mine, other, sems):
    copies = (
        pltpu.make_async_copy(mine_any, mine, sems.at[0]),
        pltpu.make_async_copy(other_any, other, sems.at[1]),
    )
    for c in copies:
        c.start()
    for c in copies:
        c.wait()
    first = 3 * (2 * lax.axis_index("y") + lax.axis_index("core"))
    g = mine[...] + other[...]
    contrib = g[0] * g[2] + g[1] * g[3]
    places = lax.broadcasted_iota(jnp.int32, (VLEN, TOK), 0)
    tokens = lax.broadcasted_iota(jnp.int32, (1, TOK), 1)
    rows = lax.broadcasted_iota(jnp.int32, (4, 3), 0)
    cols = lax.broadcasted_iota(jnp.int32, (4, 3), 1)
    result = jnp.zeros((4, 3), jnp.float32)
    for s in range(3):
        block = contrib[s * VLEN : (s + 1) * VLEN]
        per_token = jnp.sum(
            jnp.where(places < vl[first + s], block, 0.0), axis=0, keepdims=True
        )
        start = jnp.int32(0)
        for k in range(4):
            end = start + tl[0, k]
            inside = (tokens >= start) & (tokens < end)
            total = jnp.sum(
                jnp.where(inside, per_token, 0.0), axis=1, keepdims=True
            )
            result = jnp.where((rows == k) & (cols == s), total, result)
            start = end
    out[...] = result * score_scale


def scores_of(tl, vl, mine, other):
    smem = pl.BlockSpec(memory_space=pltpu.SMEM)
    any_spec = pl.BlockSpec(memory_space=pl.ANY)
    half = pltpu.VMEM((4, HALF, TOK), jnp.float32)
    return pl.pallas_call(
        score_kernel,
        out_shape=jax.ShapeDtypeStruct((4, 3), jnp.float32),
        in_specs=[smem, smem, any_spec, any_spec],
        out_specs=pl.BlockSpec(memory_space=pltpu.VMEM),
        scratch_shapes=[half, half, pltpu.SemaphoreType.DMA((2,))],
    )(tl, vl, mine, other)


def local(tx, ta, tq, to, tl, vx, va, vq, vo, vl):
    val = jnp.concatenate((vx[0], va[0], vq[0], vo[0]), axis=1)
    train = jnp.concatenate((tx, ta, tq, to), axis=1)
    dealt = jnp.stack([lax.ppermute(val, ("x", "z", "y"), deal(3 * k)) for k in range(4)])

    above, below = [train], [train]
    for _ in range(3):
        above.append(lax.ppermute(above[-1], "y", around(NY, -1)))
        below.append(lax.ppermute(below[-1], "y", around(NY, 1)))
    below.append(lax.ppermute(below[-1], "y", around(NY, 1)))
    trains = above + below[:0:-1]

    plane = jnp.concatenate(
        [dealt] + [lax.ppermute(dealt, "x", around(NX, -d)) for d in (1, 2, 3)]
    )
    up = lax.ppermute(plane, "z", around(NZ, -1))
    down = lax.ppermute(plane, "z", around(NZ, 1))
    mine, send = grams(trains, (plane, up, down))
    other = lax.ppermute(send, "core", [(0, 1), (1, 0)])
    return scores_of(tl, vl, mine, other)


def solution(mesh):
    fine = Mesh(mesh.devices.reshape(NX, NZ, NY, NC), ("x", "z", "y", "core"))
    dp, fsdp = ("x", "z"), ("y", "core")
    in_specs = (
        (P(dp, fsdp),) * 4 + (P(dp, None),) + (P(dp, None, fsdp),) * 4 + (P(),)
    )
    return jax.shard_map(
        local, mesh=fine, in_specs=in_specs, out_specs=P(dp, fsdp), check_vma=False
    )
```

```python
import jax
import jax.numpy as jnp
from jax import lax
from jax.experimental import pallas as pl
from jax.experimental.pallas import tpu as pltpu
from jax.sharding import Mesh, PartitionSpec as P

score_scale = 0.015625

NX, NZ, NY, NC = 4, 12, 8, 2
TOK, VLEN = 256, 32
SEQS = 6
ROWS = SEQS * VLEN
HALF = ROWS // 2
COLS = ((0, 256), (256, 512), (512, 896), (896, 1152))
WIDTH = 1152
MIB = 1024 * 1024

ANY = pl.BlockSpec(memory_space=pl.ANY)
VMEM = pl.BlockSpec(memory_space=pltpu.VMEM)
SMEM = pl.BlockSpec(memory_space=pltpu.SMEM)


def deal(shift):
    pairs = []
    for a in range(NY):
        for s in range(NX * NZ):
            x, z = divmod(s, NZ)
            to = x * NZ + (z - shift) % NZ
            pairs.append(((SEQS * a + s % SEQS) * NY + s // SEQS, to * NY + a))
    return pairs


def around(size, shift):
    return [(i, (i + shift) % size) for i in range(size)]


def join_kernel(tx, ta, tq, to, vx, va, vq, vo, train, val, sems):
    copies = []
    for i, (t, v, (lo, hi)) in enumerate(zip((tx, ta, tq, to), (vx, va, vq, vo), COLS)):
        copies.append(pltpu.make_async_copy(t, train.at[:, lo:hi], sems.at[2 * i]))
        copies.append(pltpu.make_async_copy(v.at[0], val.at[:, lo:hi], sems.at[2 * i + 1]))
    for c in copies:
        c.start()
    for c in copies:
        c.wait()


def join(*arrays):
    return pl.pallas_call(
        join_kernel,
        out_shape=(
            jax.ShapeDtypeStruct((TOK, WIDTH), jnp.bfloat16),
            jax.ShapeDtypeStruct((VLEN, WIDTH), jnp.bfloat16),
        ),
        in_specs=[ANY] * 8,
        out_specs=(ANY, ANY),
        scratch_shapes=[pltpu.SemaphoreType.DMA((8,))],
        compiler_params=pltpu.CompilerParams(vmem_limit_bytes=60 * MIB),
    )(*arrays)


def gram_kernel(train, c0, c1, u0, u1, d0, d1, mine, send, tbuf, vbuf, tsem, vsem):
    x, z = lax.axis_index("x"), lax.axis_index("z")
    core = lax.axis_index("core")
    vcopy = []
    for i, (near, rest) in enumerate(((c0, c1), (u0, u1), (d0, d1))):
        vcopy.append(pltpu.make_async_copy(near, vbuf.at[i, 0:4], vsem.at[2 * i]))
        vcopy.append(pltpu.make_async_copy(rest, vbuf.at[i, 4:16], vsem.at[2 * i + 1]))
    tcopy = [
        pltpu.make_async_copy(train.at[b], tbuf.at[b], tsem.at[b]) for b in range(NY)
    ]
    for c in vcopy + tcopy:
        c.start()
    for c in vcopy:
        c.wait()

    def place(b, i):
        r = i % 3 + 3 * (core if i >= 3 else 1 - core)
        s = SEQS * b + r
        dx = lax.rem(s // NZ - x + NX, NX)
        dz = lax.rem(lax.rem(s, NZ) - z + NZ, NZ)
        kind = lax.rem(dz, 3)
        step = jnp.where(kind == 2, lax.rem((dz + 1) // 3, 4), dz // 3)
        return kind, dx * 4 + step

    places = [[place(b, i) for i in range(SEQS)] for b in range(NY)]
    for g, (lo, hi) in enumerate(COLS):
        acc = None
        for b in range(NY):
            if g == 0:
                tcopy[b].wait()
            v = jnp.concatenate([vbuf[p, q, :, lo:hi] for p, q in places[b]])
            d = lax.dot_general(
                v,
                tbuf[b, :, lo:hi],
                (((1,), (1,)), ((), ())),
                preferred_element_type=jnp.float32,
            )
            acc = d if acc is None else acc + d
        send[g] = acc[:HALF]
        mine[g] = acc[HALF:]


def grams(*arrays):
    half = jax.ShapeDtypeStruct((4, HALF, TOK), jnp.float32)
    return pl.pallas_call(
        gram_kernel,
        out_shape=(half, half),
        in_specs=[ANY] * 7,
        out_specs=(VMEM, VMEM),
        scratch_shapes=[
            pltpu.VMEM((NY, TOK, WIDTH), jnp.bfloat16),
            pltpu.VMEM((3, 16, VLEN, WIDTH), jnp.bfloat16),
            pltpu.SemaphoreType.DMA((NY,)),
            pltpu.SemaphoreType.DMA((6,)),
        ],
        compiler_params=pltpu.CompilerParams(vmem_limit_bytes=GRAM_MIB * MIB),
    )(*arrays)


GRAM_MIB = 56


def score_kernel(tl, vl, mine, other, out):
    first = 3 * (2 * lax.axis_index("y") + lax.axis_index("core"))
    g = mine[...] + other[...]
    contrib = g[0] * g[2] + g[1] * g[3]
    places = lax.broadcasted_iota(jnp.int32, (VLEN, TOK), 0)
    tokens = lax.broadcasted_iota(jnp.int32, (1, TOK), 1)
    rows = lax.broadcasted_iota(jnp.int32, (4, 3), 0)
    cols = lax.broadcasted_iota(jnp.int32, (4, 3), 1)
    result = jnp.zeros((4, 3), jnp.float32)
    for s in range(3):
        block = contrib[s * VLEN : (s + 1) * VLEN]
        per_token = jnp.sum(
            jnp.where(places < vl[first + s], block, 0.0), axis=0, keepdims=True
        )
        start = jnp.int32(0)
        for k in range(4):
            end = start + tl[0, k]
            inside = (tokens >= start) & (tokens < end)
            total = jnp.sum(
                jnp.where(inside, per_token, 0.0), axis=1, keepdims=True
            )
            result = jnp.where((rows == k) & (cols == s), total, result)
            start = end
    out[...] = result * score_scale


def scores_of(tl, vl, mine, other):
    return pl.pallas_call(
        score_kernel,
        out_shape=jax.ShapeDtypeStruct((4, 3), jnp.float32),
        in_specs=[SMEM, SMEM, VMEM, VMEM],
        out_specs=VMEM,
        compiler_params=pltpu.CompilerParams(vmem_limit_bytes=16 * MIB),
    )(tl, vl, mine, other)


def local(tx, ta, tq, to, tl, vx, va, vq, vo, vl):
    train, val = join(tx, ta, tq, to, vx, va, vq, vo)
    full = lax.all_gather(train, "y", axis=0, tiled=False)
    c0 = jnp.stack([lax.ppermute(val, ("x", "z", "y"), deal(3 * k)) for k in range(4)])
    aside = [lax.ppermute(c0, "x", around(NX, -d)) for d in (1, 2, 3)]
    u0 = lax.ppermute(c0, "z", around(NZ, -1))
    d0 = lax.ppermute(c0, "z", around(NZ, 1))
    *aside, u0, d0 = lax.optimization_barrier((*aside, u0, d0))
    c1 = jnp.concatenate(aside)
    u1 = lax.ppermute(c1, "z", around(NZ, -1))
    d1 = lax.ppermute(c1, "z", around(NZ, 1))
    mine, send = grams(full, c0, c1, u0, u1, d0, d1)
    other = lax.ppermute(send, "core", [(0, 1), (1, 0)])
    return scores_of(tl, vl, mine, other)


def solution(mesh):
    fine = Mesh(mesh.devices.reshape(NX, NZ, NY, NC), ("x", "z", "y", "core"))
    dp, fsdp = ("x", "z"), ("y", "core")
    in_specs = (
        (P(dp, fsdp),) * 4 + (P(dp, None),) + (P(dp, None, fsdp),) * 4 + (P(),)
    )
    return jax.shard_map(
        local, mesh=fine, in_specs=in_specs, out_specs=P(dp, fsdp), check_vma=False
    )
```

```python
import jax
import jax.numpy as jnp
from jax import lax
from jax.experimental import pallas as pl
from jax.experimental.pallas import tpu as pltpu
from jax.sharding import Mesh, PartitionSpec as P

score_scale = 0.015625

NX, NZ, NY, NC = 4, 12, 8, 2
TOK, VLEN = 256, 32
SEQS = 6
ROWS = SEQS * VLEN
HALF = ROWS // 2
COLS = ((0, 256), (256, 512), (512, 896), (896, 1152))
WIDTH = 1152
MIB = 1024 * 1024

ANY = pl.BlockSpec(memory_space=pl.ANY)
VMEM = pl.BlockSpec(memory_space=pltpu.VMEM)
SMEM = pl.BlockSpec(memory_space=pltpu.SMEM)


SWAP = [
    ((SEQS * a + r) * NY + b, (SEQS * b + r) * NY + a)
    for a in range(NY)
    for b in range(NY)
    for r in range(SEQS)
]


def around(size, shift):
    return [(i, (i + shift) % size) for i in range(size)]


def join_kernel(tx, ta, tq, to, vx, va, vq, vo, train, val):
    for t, v, (lo, hi) in zip((tx, ta, tq, to), (vx, va, vq, vo), COLS):
        train[:, lo:hi] = t[...]
        val[:, lo:hi] = v[0]


def join(*arrays):
    return pl.pallas_call(
        join_kernel,
        out_shape=(
            jax.ShapeDtypeStruct((TOK, WIDTH), jnp.bfloat16),
            jax.ShapeDtypeStruct((VLEN, WIDTH), jnp.bfloat16),
        ),
        in_specs=[VMEM] * 8,
        out_specs=(VMEM, VMEM),
        compiler_params=pltpu.CompilerParams(vmem_limit_bytes=60 * MIB),
    )(*arrays)


def gram_kernel(train, own, right, left, far0, far1, mine, send, tbuf, vbuf, tsem, vsem):
    x = lax.axis_index("x")
    first = lax.axis_index("core") == 0
    opposite = lax.rem(x + 2, NX)
    vcopy = [
        pltpu.make_async_copy(src, dst, vsem.at[i])
        for i, (src, dst) in enumerate(
            (
                (own, vbuf.at[x]),
                (right, vbuf.at[lax.rem(x + 1, NX)]),
                (left, vbuf.at[lax.rem(x + 3, NX)]),
                (far0, vbuf.at[opposite, 0:ROWS]),
                (far1, vbuf.at[opposite, ROWS : 2 * ROWS]),
            )
        )
    ]
    tcopy = [
        pltpu.make_async_copy(train.at[:, :, lo:hi], tbuf.at[:, :, lo:hi], tsem.at[g])
        for g, (lo, hi) in enumerate(COLS)
    ]
    for c in (*tcopy, *vcopy):
        c.start()
    for c in vcopy:
        c.wait()
    for g, (lo, hi) in enumerate(COLS):
        tcopy[g].wait()
        acc = jnp.zeros((ROWS, TOK), jnp.float32)
        for b in range(NY):
            acc += lax.dot_general(
                vbuf[b // 2, (b % 2) * ROWS : (b % 2 + 1) * ROWS, lo:hi],
                tbuf[b, :, lo:hi],
                (((1,), (1,)), ((), ())),
                preferred_element_type=jnp.float32,
            )
        send[g] = jnp.where(first, acc[HALF:], acc[:HALF])
        mine[g] = jnp.where(first, acc[:HALF], acc[HALF:])


def grams(*arrays):
    half = jax.ShapeDtypeStruct((4, HALF, TOK), jnp.float32)
    return pl.pallas_call(
        gram_kernel,
        out_shape=(half, half),
        in_specs=[ANY] * 6,
        out_specs=(VMEM, VMEM),
        scratch_shapes=[
            pltpu.VMEM((NY, TOK, WIDTH), jnp.bfloat16),
            pltpu.VMEM((NX, 2 * ROWS, WIDTH), jnp.bfloat16),
            pltpu.SemaphoreType.DMA((4,)),
            pltpu.SemaphoreType.DMA((5,)),
        ],
        compiler_params=pltpu.CompilerParams(vmem_limit_bytes=GRAM_MIB * MIB),
    )(*arrays)


GRAM_MIB = 50


def score_kernel(tl, vl, mine, other, out):
    first = 3 * (2 * lax.axis_index("y") + lax.axis_index("core"))
    g = mine[...] + other[...]
    contrib = g[0] * g[2] + g[1] * g[3]
    places = lax.broadcasted_iota(jnp.int32, (VLEN, TOK), 0)
    tokens = lax.broadcasted_iota(jnp.int32, (1, TOK), 1)
    rows = lax.broadcasted_iota(jnp.int32, (4, 3), 0)
    cols = lax.broadcasted_iota(jnp.int32, (4, 3), 1)
    result = jnp.zeros((4, 3), jnp.float32)
    for s in range(3):
        block = contrib[s * VLEN : (s + 1) * VLEN]
        per_token = jnp.sum(
            jnp.where(places < vl[first + s], block, 0.0), axis=0, keepdims=True
        )
        start = jnp.int32(0)
        for k in range(4):
            end = start + tl[0, k]
            inside = (tokens >= start) & (tokens < end)
            total = jnp.sum(
                jnp.where(inside, per_token, 0.0), axis=1, keepdims=True
            )
            result = jnp.where((rows == k) & (cols == s), total, result)
            start = end
    out[...] = result * score_scale


def scores_of(tl, vl, mine, other):
    return pl.pallas_call(
        score_kernel,
        out_shape=jax.ShapeDtypeStruct((4, 3), jnp.float32),
        in_specs=[SMEM, SMEM, VMEM, VMEM],
        out_specs=VMEM,
        compiler_params=pltpu.CompilerParams(vmem_limit_bytes=16 * MIB),
    )(tl, vl, mine, other)


def local(tx, ta, tq, to, tl, vx, va, vq, vo, vl):
    train, val = join(tx, ta, tq, to, vx, va, vq, vo)
    full = lax.all_gather(train, "y", axis=0, tiled=False)
    val = lax.ppermute(val, ("x", "z", "y"), SWAP)
    own = lax.all_gather(val, "z", axis=0, tiled=True)
    right = lax.ppermute(own, "x", around(NX, -1))
    left = lax.ppermute(own, "x", around(NX, 1))
    far0 = lax.ppermute(left[:ROWS], "x", around(NX, 1))
    far1 = lax.ppermute(right[ROWS:], "x", around(NX, -1))
    mine, send = grams(full, own, right, left, far0, far1)
    other = lax.ppermute(send, "core", [(0, 1), (1, 0)])
    return scores_of(tl, vl, mine, other)


def solution(mesh):
    fine = Mesh(mesh.devices.reshape(NX, NZ, NY, NC), ("x", "z", "y", "core"))
    dp, fsdp = ("x", "z"), ("y", "core")
    in_specs = (
        (P(dp, fsdp),) * 4 + (P(dp, None),) + (P(dp, None, fsdp),) * 4 + (P(),)
    )
    return jax.shard_map(
        local, mesh=fine, in_specs=in_specs, out_specs=P(dp, fsdp), check_vma=False
    )
```

```python
import functools

import jax
import jax.numpy as jnp
from jax import lax
from jax.experimental import pallas as pl
from jax.experimental.pallas import tpu as pltpu
from jax.sharding import Mesh, PartitionSpec as P

score_scale = 0.015625

NX, NZ, NY, NC = 4, 12, 8, 2
TOK, VLEN = 256, 32
SEQS = 6
ROWS = SEQS * VLEN
HALF = ROWS // 2
COLS = ((0, 256), (256, 512), (512, 896), (896, 1152))
WIDTH = 1152
MIB = 1024 * 1024

ANY = pl.BlockSpec(memory_space=pl.ANY)
VMEM = pl.BlockSpec(memory_space=pltpu.VMEM)
SMEM = pl.BlockSpec(memory_space=pltpu.SMEM)


SWAP = [
    ((SEQS * a + r) * NY + b, (SEQS * b + r) * NY + a)
    for a in range(NY)
    for b in range(NY)
    for r in range(SEQS)
]


def around(size, shift):
    return [(i, (i + shift) % size) for i in range(size)]


def join_kernel(tx, ta, tq, to, vx, va, vq, vo, train, val):
    for t, v, (lo, hi) in zip((tx, ta, tq, to), (vx, va, vq, vo), COLS):
        train[:, lo:hi] = t[...]
        val[:, lo:hi] = v[0]


def join(*arrays):
    return pl.pallas_call(
        join_kernel,
        out_shape=(
            jax.ShapeDtypeStruct((TOK, WIDTH), jnp.bfloat16),
            jax.ShapeDtypeStruct((VLEN, WIDTH), jnp.bfloat16),
        ),
        in_specs=[VMEM] * 8,
        out_specs=(VMEM, VMEM),
        compiler_params=pltpu.CompilerParams(vmem_limit_bytes=60 * MIB),
    )(*arrays)


NEAR = ((0, 2 * ROWS), (1, 2 * ROWS), (3, 2 * ROWS))
FAR = ((2, ROWS), (2, ROWS))


def gram_kernel(pieces, *refs):
    n = len(pieces)
    count = sum(rows for _, rows in pieces) // ROWS
    train, vals, rest = refs[0], refs[1 : n + 1], refs[n + 1 :]
    before, (mine, send, tbuf, vbuf, tsem, vsem) = rest[:-6], rest[-6:]
    x = lax.axis_index("x")
    first = lax.axis_index("core") == 0
    tcopy, vcopy, j = [], [], 0
    for i, (ref, (shift, rows)) in enumerate(zip(vals, pieces)):
        blocks = rows // ROWS
        vcopy.append(
            pltpu.make_async_copy(ref, vbuf.at[pl.ds(j * ROWS, rows)], vsem.at[i])
        )
        for h in range(blocks):
            b = 2 * lax.rem(x + shift, NX) + (h if blocks == 2 else i)
            tcopy.append(pltpu.make_async_copy(train.at[b], tbuf.at[j], tsem.at[j]))
            j += 1
    for c in (*vcopy, *tcopy):
        c.start()
    for c in vcopy:
        c.wait()
    for g, (lo, hi) in enumerate(COLS):
        acc = None
        for j in range(count):
            if g == 0:
                tcopy[j].wait()
            d = lax.dot_general(
                vbuf[j * ROWS : (j + 1) * ROWS, lo:hi],
                tbuf[j, :, lo:hi],
                (((1,), (1,)), ((), ())),
                preferred_element_type=jnp.float32,
            )
            acc = d if acc is None else acc + d
        keep = jnp.where(first, acc[:HALF], acc[HALF:])
        give = jnp.where(first, acc[HALF:], acc[:HALF])
        if before:
            keep, give = keep + before[0][g], give + before[1][g]
        mine[g] = keep
        send[g] = give


def grams(pieces, train, vals, before=()):
    half = jax.ShapeDtypeStruct((4, HALF, TOK), jnp.float32)
    count = sum(rows for _, rows in pieces) // ROWS
    return pl.pallas_call(
        functools.partial(gram_kernel, pieces),
        out_shape=(half, half),
        in_specs=[ANY] * (1 + len(pieces)) + [VMEM] * len(before),
        out_specs=(VMEM, VMEM),
        scratch_shapes=[
            pltpu.VMEM((count, TOK, WIDTH), jnp.bfloat16),
            pltpu.VMEM((count * ROWS, WIDTH), jnp.bfloat16),
            pltpu.SemaphoreType.DMA((count,)),
            pltpu.SemaphoreType.DMA((len(pieces),)),
        ],
        compiler_params=pltpu.CompilerParams(vmem_limit_bytes=GRAM_MIB * MIB),
        cost_estimate=pl.CostEstimate(
            flops=2 * count * ROWS * TOK * WIDTH,
            bytes_accessed=2 * count * (ROWS + TOK) * WIDTH,
            transcendentals=0,
        ),
    )(train, *vals, *before)


GRAM_MIB = 48


def score_kernel(tl, vl, mine, other, out):
    first = 3 * (2 * lax.axis_index("y") + lax.axis_index("core"))
    g = mine[...] + other[...]
    contrib = g[0] * g[2] + g[1] * g[3]
    places = lax.broadcasted_iota(jnp.int32, (VLEN, TOK), 0)
    tokens = lax.broadcasted_iota(jnp.int32, (1, TOK), 1)
    rows = lax.broadcasted_iota(jnp.int32, (4, 3), 0)
    cols = lax.broadcasted_iota(jnp.int32, (4, 3), 1)
    result = jnp.zeros((4, 3), jnp.float32)
    for s in range(3):
        block = contrib[s * VLEN : (s + 1) * VLEN]
        per_token = jnp.sum(
            jnp.where(places < vl[first + s], block, 0.0), axis=0, keepdims=True
        )
        start = jnp.int32(0)
        for k in range(4):
            end = start + tl[0, k]
            inside = (tokens >= start) & (tokens < end)
            total = jnp.sum(
                jnp.where(inside, per_token, 0.0), axis=1, keepdims=True
            )
            result = jnp.where((rows == k) & (cols == s), total, result)
            start = end
    out[...] = result * score_scale


def scores_of(tl, vl, mine, other):
    return pl.pallas_call(
        score_kernel,
        out_shape=jax.ShapeDtypeStruct((4, 3), jnp.float32),
        in_specs=[SMEM, SMEM, VMEM, VMEM],
        out_specs=VMEM,
        compiler_params=pltpu.CompilerParams(vmem_limit_bytes=16 * MIB),
    )(tl, vl, mine, other)


def local(tx, ta, tq, to, tl, vx, va, vq, vo, vl):
    train, val = join(tx, ta, tq, to, vx, va, vq, vo)
    full = lax.all_gather(train, "y", axis=0, tiled=False)
    val = lax.ppermute(val, ("x", "z", "y"), SWAP)
    own = lax.all_gather(val, "z", axis=0, tiled=True)
    right = lax.ppermute(own, "x", around(NX, -1))
    left = lax.ppermute(own, "x", around(NX, 1))
    far0 = lax.ppermute(left[:ROWS], "x", around(NX, 1))
    far1 = lax.ppermute(right[ROWS:], "x", around(NX, -1))
    near = grams(NEAR, full, (own, right, left))
    mine, send = grams(FAR, full, (far0, far1), near)
    other = lax.ppermute(send, "core", [(0, 1), (1, 0)])
    return scores_of(tl, vl, mine, other)


def solution(mesh):
    fine = Mesh(mesh.devices.reshape(NX, NZ, NY, NC), ("x", "z", "y", "core"))
    dp, fsdp = ("x", "z"), ("y", "core")
    in_specs = (
        (P(dp, fsdp),) * 4 + (P(dp, None),) + (P(dp, None, fsdp),) * 4 + (P(),)
    )
    return jax.shard_map(
        local, mesh=fine, in_specs=in_specs, out_specs=P(dp, fsdp), check_vma=False
    )
```

```python
import functools

import jax
import jax.numpy as jnp
from jax import lax
from jax.experimental import pallas as pl
from jax.experimental.pallas import tpu as pltpu
from jax.sharding import Mesh, PartitionSpec as P

score_scale = 0.015625

NX, NZ, NQ, NL, NC = 4, 12, 4, 2, 2
NY = NQ * NL
TOK, VLEN = 256, 32
WIDTH = 640
COLS = ((0, 256), (256, 640))
HALF = 3 * VLEN
GROUP = NZ // 2 * VLEN
MIB = 1024 * 1024

ANY = pl.BlockSpec(memory_space=pl.ANY)
VMEM = pl.BlockSpec(memory_space=pltpu.VMEM)
SMEM = pl.BlockSpec(memory_space=pltpu.SMEM)

CHIP = ("x", "z", "yh", "yl")


def swap(other):
    return [
        (
            ((x * NZ + z) * NQ + q) * NL + l,
            ((q * NZ + z) * NQ + x) * NL + (1 - l if other else l),
        )
        for x in range(NX)
        for z in range(NZ)
        for q in range(NQ)
        for l in range(NL)
    ]


def around(size, shift):
    return [(i, (i + shift) % size) for i in range(size)]


def join_kernel(tx, ta, tq, to, vx, va, vq, vo, parts, same, other, xq, ao, sems):
    xq[:, :256] = tx[...]
    xq[:, 256:] = tq[...]
    ao[:, :256] = ta[...]
    ao[:, 256:512] = to[...]
    ao[:, 512:] = jnp.zeros((TOK, 128), jnp.bfloat16)
    copies = [
        pltpu.make_async_copy(ao if y % 2 else xq, parts.at[y], sems.at[y])
        for y in range(NY)
    ]
    for c in copies:
        c.start()
    even = lax.axis_index("yl") == 0
    vxq = (vx[0], vq[0])
    vao = (va[0], jnp.concatenate((vo[0], jnp.zeros((VLEN, 128), jnp.bfloat16)), 1))
    for (lo, hi), p, q in zip(COLS, vxq, vao):
        same[:, lo:hi] = jnp.where(even, p, q)
        other[:, lo:hi] = jnp.where(even, q, p)
    for c in copies:
        c.wait()


def join(*arrays):
    block = jax.ShapeDtypeStruct((VLEN, WIDTH), jnp.bfloat16)
    whole = pltpu.VMEM((TOK, WIDTH), jnp.bfloat16)
    return pl.pallas_call(
        join_kernel,
        out_shape=(
            jax.ShapeDtypeStruct((NY, TOK, WIDTH), jnp.bfloat16),
            block,
            block,
        ),
        in_specs=[VMEM] * 8,
        out_specs=(ANY, VMEM, VMEM),
        scratch_shapes=[whole, whole, pltpu.SemaphoreType.DMA((NY,))],
        compiler_params=pltpu.CompilerParams(vmem_limit_bytes=58 * MIB),
    )(*arrays)


NEAR = ((0, 0, 12), (1, 0, 12), (3, 0, 12))
FAR = ((2, 0, 6), (2, 6, 12))


def gram_kernel(pieces, *refs):
    n = len(pieces)
    shifts = sorted({shift for shift, _, _ in pieces})
    train, vals, rest = refs[0], refs[1 : n + 1], refs[n + 1 :]
    before, (mine, send, tbuf, vbuf, tsem, vsem) = rest[:-6], rest[-6:]
    x, l = lax.axis_index("x"), lax.axis_index("yl")
    first = lax.axis_index("core") == 0
    tcopy = []
    for k, shift in enumerate(shifts):
        q = lax.rem(x + shift, NX)
        for e in range(2):
            y = 2 * q + (l if e == 0 else 1 - l)
            j = 2 * k + e
            tcopy.append(pltpu.make_async_copy(train.at[y], tbuf.at[j], tsem.at[j]))
    vcopy = [
        pltpu.make_async_copy(ref, vbuf.at[shifts.index(shift), lo:hi], vsem.at[i])
        for i, (ref, (shift, lo, hi)) in enumerate(zip(vals, pieces))
    ]
    for c in (*vcopy, *tcopy):
        c.start()
    for c in (*vcopy, *tcopy):
        c.wait()
    for g, (lo, hi) in enumerate(COLS):
        for m in range(2):
            acc = None
            for j in range(2 * len(shifts)):
                v = vbuf[j // 2, 6 * m : 6 * m + 6, j % 2, :, lo:hi]
                d = lax.dot_general(
                    v.reshape(GROUP, hi - lo),
                    tbuf[j, :, lo:hi],
                    (((1,), (1,)), ((), ())),
                    preferred_element_type=jnp.float32,
                )
                acc = d if acc is None else acc + d
            keep = jnp.where(first, acc[:HALF], acc[HALF:])
            give = jnp.where(first, acc[HALF:], acc[:HALF])
            if before:
                keep, give = keep + before[0][g, m], give + before[1][g, m]
            mine[g, m] = keep
            send[g, m] = give


def grams(pieces, train, vals, before=()):
    half = jax.ShapeDtypeStruct((2, 2, HALF, TOK), jnp.float32)
    count = len({shift for shift, _, _ in pieces})
    return pl.pallas_call(
        functools.partial(gram_kernel, pieces),
        out_shape=(half, half),
        in_specs=[ANY] * (1 + len(pieces)) + [VMEM] * len(before),
        out_specs=(VMEM, VMEM),
        scratch_shapes=[
            pltpu.VMEM((2 * count, TOK, WIDTH), jnp.bfloat16),
            pltpu.VMEM((count, NZ, 2, VLEN, WIDTH), jnp.bfloat16),
            pltpu.SemaphoreType.DMA((2 * count,)),
            pltpu.SemaphoreType.DMA((len(pieces),)),
        ],
        compiler_params=pltpu.CompilerParams(vmem_limit_bytes=GRAM_MIB * MIB),
        cost_estimate=pl.CostEstimate(
            flops=4 * count * NZ * VLEN * TOK * WIDTH,
            bytes_accessed=4 * count * (NZ * VLEN + TOK) * WIDTH,
            transcendentals=0,
        ),
    )(train, *vals, *before)


GRAM_MIB = 16


def score_kernel(tl, vl, mine, other, keep, give):
    core, l = lax.axis_index("core"), lax.axis_index("yl")
    g = mine[...] + other[...]
    contrib = g[0] * g[1]
    places = lax.broadcasted_iota(jnp.int32, (VLEN, TOK), 0)
    tokens = lax.broadcasted_iota(jnp.int32, (1, TOK), 1)
    rows = lax.broadcasted_iota(jnp.int32, (4, 3), 0)
    cols = lax.broadcasted_iota(jnp.int32, (4, 3), 1)
    results = []
    for m in range(2):
        first = NZ * lax.axis_index("yh") + 6 * m + 3 * core
        result = jnp.zeros((4, 3), jnp.float32)
        for s in range(3):
            block = contrib[m, s * VLEN : (s + 1) * VLEN]
            per_token = jnp.sum(
                jnp.where(places < vl[first + s], block, 0.0), axis=0, keepdims=True
            )
            start = jnp.int32(0)
            for k in range(4):
                end = start + tl[0, k]
                inside = (tokens >= start) & (tokens < end)
                total = jnp.sum(
                    jnp.where(inside, per_token, 0.0), axis=1, keepdims=True
                )
                result = jnp.where((rows == k) & (cols == s), total, result)
                start = end
        results.append(result * score_scale)
    keep[...] = jnp.where(l == 0, results[0], results[1])
    give[...] = jnp.where(l == 0, results[1], results[0])


def scores_of(tl, vl, mine, other):
    part = jax.ShapeDtypeStruct((4, 3), jnp.float32)
    return pl.pallas_call(
        score_kernel,
        out_shape=(part, part),
        in_specs=[SMEM, SMEM, VMEM, VMEM],
        out_specs=(VMEM, VMEM),
        compiler_params=pltpu.CompilerParams(vmem_limit_bytes=16 * MIB),
    )(tl, vl, mine, other)


def local(tx, ta, tq, to, tl, vx, va, vq, vo, vl):
    parts, same, other = join(tx, ta, tq, to, vx, va, vq, vo)
    train = lax.all_to_all(parts, ("yh", "yl"), 0, 0, tiled=True)
    val = jnp.stack(
        (
            lax.ppermute(same, CHIP, swap(False)),
            lax.ppermute(other, CHIP, swap(True)),
        )
    )
    own = lax.all_gather(val, "z", axis=0, tiled=False)
    right = lax.ppermute(own, "x", around(NX, -1))
    left = lax.ppermute(own, "x", around(NX, 1))
    far0 = lax.ppermute(left[:6], "x", around(NX, 1))
    far1 = lax.ppermute(right[6:], "x", around(NX, -1))
    near = grams(NEAR, train, (own, right, left))
    mine, send = grams(FAR, train, (far0, far1), near)
    theirs = lax.ppermute(send, "core", [(0, 1), (1, 0)])
    keep, give = scores_of(tl, vl, mine, theirs)
    return keep + lax.ppermute(give, "yl", [(0, 1), (1, 0)])


def solution(mesh):
    fine = Mesh(
        mesh.devices.reshape(NX, NZ, NQ, NL, NC), ("x", "z", "yh", "yl", "core")
    )
    dp, fsdp = ("x", "z"), ("yh", "yl", "core")
    in_specs = (
        (P(dp, fsdp),) * 4 + (P(dp, None),) + (P(dp, None, fsdp),) * 4 + (P(),)
    )
    return jax.shard_map(
        local, mesh=fine, in_specs=in_specs, out_specs=P(dp, fsdp), check_vma=False
    )
```

```python
import functools

import jax
import jax.numpy as jnp
from jax import lax
from jax.experimental import pallas as pl
from jax.experimental.pallas import tpu as pltpu
from jax.sharding import Mesh, PartitionSpec as P

score_scale = 0.015625

NX, NZ, NY, NC = 4, 12, 8, 2
TOK, VLEN = 256, 32
SEQS = 6
ROWS = SEQS * VLEN
HALF = ROWS // 2
COLS = ((0, 256), (256, 512), (512, 896), (896, 1152))
WIDTH = 1152
MIB = 1024 * 1024

ANY = pl.BlockSpec(memory_space=pl.ANY)
VMEM = pl.BlockSpec(memory_space=pltpu.VMEM)
SMEM = pl.BlockSpec(memory_space=pltpu.SMEM)


SWAP = [
    ((SEQS * a + r) * NY + b, (SEQS * b + r) * NY + a)
    for a in range(NY)
    for b in range(NY)
    for r in range(SEQS)
]


def around(size, shift):
    return [(i, (i + shift) % size) for i in range(size)]


def join_kernel(tx, ta, tq, to, vx, va, vq, vo, train, val):
    for t, v, (lo, hi) in zip((tx, ta, tq, to), (vx, va, vq, vo), COLS):
        train[:, lo:hi] = t[...]
        val[:, lo:hi] = v[0]


def join(*arrays):
    return pl.pallas_call(
        join_kernel,
        out_shape=(
            jax.ShapeDtypeStruct((TOK, WIDTH), jnp.bfloat16),
            jax.ShapeDtypeStruct((VLEN, WIDTH), jnp.bfloat16),
        ),
        in_specs=[VMEM] * 8,
        out_specs=(VMEM, VMEM),
        compiler_params=pltpu.CompilerParams(vmem_limit_bytes=60 * MIB),
    )(*arrays)


def gram_kernel(shifts, *refs):
    count = 2 * len(shifts)
    train, vals, rest = refs[0], refs[1], refs[2:]
    before, (mine, send, tbuf, vbuf, tsem, vsem) = rest[:-6], rest[-6:]
    x = lax.axis_index("x")
    first = lax.axis_index("core") == 0
    tcopy, vcopy = [], []
    for i, shift in enumerate(shifts):
        at = lax.rem(x + shift, NX)
        source = vals.at[at] if before else vals
        vcopy.append(pltpu.make_async_copy(source, vbuf.at[i], vsem.at[i]))
        for h in range(2):
            j = 2 * i + h
            tcopy.append(
                pltpu.make_async_copy(train.at[2 * at + h], tbuf.at[j], tsem.at[j])
            )
    for c in (*vcopy, *tcopy):
        c.start()
    for c in vcopy:
        c.wait()
    for g, (lo, hi) in enumerate(COLS):
        acc = None
        for j in range(count):
            if g == 0:
                tcopy[j].wait()
            d = lax.dot_general(
                vbuf[j // 2, (j % 2) * ROWS : (j % 2 + 1) * ROWS, lo:hi],
                tbuf[j, :, lo:hi],
                (((1,), (1,)), ((), ())),
                preferred_element_type=jnp.float32,
            )
            acc = d if acc is None else acc + d
        keep = jnp.where(first, acc[:HALF], acc[HALF:])
        give = jnp.where(first, acc[HALF:], acc[:HALF])
        if before:
            keep, give = keep + before[0][g], give + before[1][g]
        mine[g] = keep
        send[g] = give


def grams(shifts, train, vals, before=()):
    half = jax.ShapeDtypeStruct((4, HALF, TOK), jnp.float32)
    n = len(shifts)
    return pl.pallas_call(
        functools.partial(gram_kernel, shifts),
        out_shape=(half, half),
        in_specs=[ANY] * 2 + [VMEM] * len(before),
        out_specs=(VMEM, VMEM),
        scratch_shapes=[
            pltpu.VMEM((2 * n, TOK, WIDTH), jnp.bfloat16),
            pltpu.VMEM((n, 2 * ROWS, WIDTH), jnp.bfloat16),
            pltpu.SemaphoreType.DMA((2 * n,)),
            pltpu.SemaphoreType.DMA((n,)),
        ],
        compiler_params=pltpu.CompilerParams(vmem_limit_bytes=GRAM_MIB * MIB),
        cost_estimate=pl.CostEstimate(
            flops=4 * n * ROWS * TOK * WIDTH,
            bytes_accessed=4 * n * (ROWS + TOK) * WIDTH,
            transcendentals=0,
        ),
    )(train, vals, *before)


GRAM_MIB = 50


def score_kernel(tl, vl, mine, other, out):
    first = 3 * (2 * lax.axis_index("y") + lax.axis_index("core"))
    g = mine[...] + other[...]
    contrib = g[0] * g[2] + g[1] * g[3]
    places = lax.broadcasted_iota(jnp.int32, (VLEN, TOK), 0)
    tokens = lax.broadcasted_iota(jnp.int32, (1, TOK), 1)
    rows = lax.broadcasted_iota(jnp.int32, (4, 3), 0)
    cols = lax.broadcasted_iota(jnp.int32, (4, 3), 1)
    result = jnp.zeros((4, 3), jnp.float32)
    for s in range(3):
        block = contrib[s * VLEN : (s + 1) * VLEN]
        per_token = jnp.sum(
            jnp.where(places < vl[first + s], block, 0.0), axis=0, keepdims=True
        )
        start = jnp.int32(0)
        for k in range(4):
            end = start + tl[0, k]
            inside = (tokens >= start) & (tokens < end)
            total = jnp.sum(
                jnp.where(inside, per_token, 0.0), axis=1, keepdims=True
            )
            result = jnp.where((rows == k) & (cols == s), total, result)
            start = end
    out[...] = result * score_scale


def scores_of(tl, vl, mine, other):
    return pl.pallas_call(
        score_kernel,
        out_shape=jax.ShapeDtypeStruct((4, 3), jnp.float32),
        in_specs=[SMEM, SMEM, VMEM, VMEM],
        out_specs=VMEM,
        compiler_params=pltpu.CompilerParams(vmem_limit_bytes=16 * MIB),
    )(tl, vl, mine, other)


def local(tx, ta, tq, to, tl, vx, va, vq, vo, vl):
    train, val = join(tx, ta, tq, to, vx, va, vq, vo)
    full = lax.all_gather(train, "y", axis=0, tiled=False)
    val = lax.ppermute(val, ("x", "z", "y"), SWAP)
    own = lax.all_gather(val, "z", axis=0, tiled=True)
    copies = jnp.broadcast_to(own[None], (NX, 2 * ROWS, WIDTH))
    plane = lax.all_to_all(copies, "x", 0, 0, tiled=True)
    near = grams((0,), full, own)
    mine, send = grams((1, 3, 2), full, plane, near)
    other = lax.ppermute(send, "core", [(0, 1), (1, 0)])
    return scores_of(tl, vl, mine, other)


def solution(mesh):
    fine = Mesh(mesh.devices.reshape(NX, NZ, NY, NC), ("x", "z", "y", "core"))
    dp, fsdp = ("x", "z"), ("y", "core")
    in_specs = (
        (P(dp, fsdp),) * 4 + (P(dp, None),) + (P(dp, None, fsdp),) * 4 + (P(),)
    )
    return jax.shard_map(
        local, mesh=fine, in_specs=in_specs, out_specs=P(dp, fsdp), check_vma=False
    )
```

```python
import functools

import jax
import jax.numpy as jnp
from jax import lax
from jax.experimental import pallas as pl
from jax.experimental.pallas import tpu as pltpu
from jax.sharding import Mesh, PartitionSpec as P

score_scale = 0.015625

NX, NZ, NY, NC = 4, 12, 8, 2
TOK, VLEN = 256, 32
SEQS = 6
ROWS = SEQS * VLEN
HALF = ROWS // 2
COLS = ((0, 256), (256, 512), (512, 896), (896, 1152))
WIDTH = 1152
MIB = 1024 * 1024

ANY = pl.BlockSpec(memory_space=pl.ANY)
VMEM = pl.BlockSpec(memory_space=pltpu.VMEM)
SMEM = pl.BlockSpec(memory_space=pltpu.SMEM)


SWAP = [
    ((SEQS * a + r) * NY + b, (SEQS * b + r) * NY + a)
    for a in range(NY)
    for b in range(NY)
    for r in range(SEQS)
]


def around(size, shift):
    return [(i, (i + shift) % size) for i in range(size)]


APART = [
    (x * NC + c, (x + (-1 if c else 1)) % NX * NC + c)
    for x in range(NX)
    for c in range(NC)
]


def join_kernel(tx, ta, tq, to, vx, va, vq, vo, train, val):
    for t, v, (lo, hi) in zip((tx, ta, tq, to), (vx, va, vq, vo), COLS):
        train[:, lo:hi] = t[...]
        val[:, lo:hi] = v[0]


def join(*arrays):
    return pl.pallas_call(
        join_kernel,
        out_shape=(
            jax.ShapeDtypeStruct((TOK, WIDTH), jnp.bfloat16),
            jax.ShapeDtypeStruct((VLEN, WIDTH), jnp.bfloat16),
        ),
        in_specs=[VMEM] * 8,
        out_specs=(VMEM, VMEM),
        compiler_params=pltpu.CompilerParams(vmem_limit_bytes=60 * MIB),
    )(*arrays)


NEAR = ((0, 2 * ROWS), (1, 2 * ROWS), (3, 2 * ROWS))
FAR = ((2, 2 * ROWS),)


def gram_kernel(pieces, *refs):
    n = len(pieces)
    count = sum(rows for _, rows in pieces) // ROWS
    train, vals, rest = refs[0], refs[1 : n + 1], refs[n + 1 :]
    before, (mine, send, tbuf, vbuf, tsem, vsem) = rest[:-6], rest[-6:]
    x = lax.axis_index("x")
    first = lax.axis_index("core") == 0
    tcopy, vcopy, j = [], [], 0
    for i, (ref, (shift, rows)) in enumerate(zip(vals, pieces)):
        blocks = rows // ROWS
        vcopy.append(
            pltpu.make_async_copy(ref, vbuf.at[pl.ds(j * ROWS, rows)], vsem.at[i])
        )
        for h in range(blocks):
            b = 2 * lax.rem(x + shift, NX) + (h if blocks == 2 else i)
            tcopy.append(pltpu.make_async_copy(train.at[b], tbuf.at[j], tsem.at[j]))
            j += 1
    for c in (*vcopy, *tcopy):
        c.start()
    for c in vcopy:
        c.wait()
    for g, (lo, hi) in enumerate(COLS):
        acc = None
        for j in range(count):
            if g == 0:
                tcopy[j].wait()
            d = lax.dot_general(
                vbuf[j * ROWS : (j + 1) * ROWS, lo:hi],
                tbuf[j, :, lo:hi],
                (((1,), (1,)), ((), ())),
                preferred_element_type=jnp.float32,
            )
            acc = d if acc is None else acc + d
        keep = jnp.where(first, acc[:HALF], acc[HALF:])
        give = jnp.where(first, acc[HALF:], acc[:HALF])
        if before:
            keep, give = keep + before[0][g], give + before[1][g]
        mine[g] = keep
        send[g] = give


def grams(pieces, train, vals, before=()):
    half = jax.ShapeDtypeStruct((4, HALF, TOK), jnp.float32)
    count = sum(rows for _, rows in pieces) // ROWS
    return pl.pallas_call(
        functools.partial(gram_kernel, pieces),
        out_shape=(half, half),
        in_specs=[ANY] * (1 + len(pieces)) + [VMEM] * len(before),
        out_specs=(VMEM, VMEM),
        scratch_shapes=[
            pltpu.VMEM((count, TOK, WIDTH), jnp.bfloat16),
            pltpu.VMEM((count * ROWS, WIDTH), jnp.bfloat16),
            pltpu.SemaphoreType.DMA((count,)),
            pltpu.SemaphoreType.DMA((len(pieces),)),
        ],
        compiler_params=pltpu.CompilerParams(vmem_limit_bytes=GRAM_MIB * MIB),
        cost_estimate=pl.CostEstimate(
            flops=2 * count * ROWS * TOK * WIDTH,
            bytes_accessed=2 * count * (ROWS + TOK) * WIDTH,
            transcendentals=0,
        ),
    )(train, *vals, *before)


GRAM_MIB = 48


def score_kernel(tl, vl, mine, other, out):
    first = 3 * (2 * lax.axis_index("y") + lax.axis_index("core"))
    g = mine[...] + other[...]
    contrib = g[0] * g[2] + g[1] * g[3]
    places = lax.broadcasted_iota(jnp.int32, (VLEN, TOK), 0)
    tokens = lax.broadcasted_iota(jnp.int32, (1, TOK), 1)
    rows = lax.broadcasted_iota(jnp.int32, (4, 3), 0)
    cols = lax.broadcasted_iota(jnp.int32, (4, 3), 1)
    result = jnp.zeros((4, 3), jnp.float32)
    for s in range(3):
        block = contrib[s * VLEN : (s + 1) * VLEN]
        per_token = jnp.sum(
            jnp.where(places < vl[first + s], block, 0.0), axis=0, keepdims=True
        )
        start = jnp.int32(0)
        for k in range(4):
            end = start + tl[0, k]
            inside = (tokens >= start) & (tokens < end)
            total = jnp.sum(
                jnp.where(inside, per_token, 0.0), axis=1, keepdims=True
            )
            result = jnp.where((rows == k) & (cols == s), total, result)
            start = end
    out[...] = result * score_scale


def scores_of(tl, vl, mine, other):
    return pl.pallas_call(
        score_kernel,
        out_shape=jax.ShapeDtypeStruct((4, 3), jnp.float32),
        in_specs=[SMEM, SMEM, VMEM, VMEM],
        out_specs=VMEM,
        compiler_params=pltpu.CompilerParams(vmem_limit_bytes=16 * MIB),
    )(tl, vl, mine, other)


def local(tx, ta, tq, to, tl, vx, va, vq, vo, vl):
    train, val = join(tx, ta, tq, to, vx, va, vq, vo)
    full = lax.all_gather(train, "y", axis=0, tiled=False)
    val = lax.ppermute(val, ("x", "z", "y"), SWAP)
    own = lax.all_gather(val, "z", axis=0, tiled=True)
    right = lax.ppermute(own, "x", around(NX, -1))
    left = lax.ppermute(own, "x", around(NX, 1))
    onward = lax.select(lax.axis_index("core") == 0, left, right)
    far = lax.ppermute(onward, ("x", "core"), APART)
    near = grams(NEAR, full, (own, right, left))
    mine, send = grams(FAR, full, (far,), near)
    other = lax.ppermute(send, "core", [(0, 1), (1, 0)])
    return scores_of(tl, vl, mine, other)


def solution(mesh):
    fine = Mesh(mesh.devices.reshape(NX, NZ, NY, NC), ("x", "z", "y", "core"))
    dp, fsdp = ("x", "z"), ("y", "core")
    in_specs = (
        (P(dp, fsdp),) * 4 + (P(dp, None),) + (P(dp, None, fsdp),) * 4 + (P(),)
    )
    return jax.shard_map(
        local, mesh=fine, in_specs=in_specs, out_specs=P(dp, fsdp), check_vma=False
    )
```

```python
import functools

import jax
import jax.numpy as jnp
from jax import lax
from jax.experimental import pallas as pl
from jax.experimental.pallas import tpu as pltpu
from jax.sharding import Mesh, PartitionSpec as P

score_scale = 0.015625

NX, NZ, NY, NC = 4, 12, 8, 2
TOK, VLEN = 256, 32
SEQS = 6
ROWS = SEQS * VLEN
HALF = ROWS // 2
COLS = ((0, 256), (256, 512), (512, 896), (896, 1152))
WIDTH = 1152
MIB = 1024 * 1024

ANY = pl.BlockSpec(memory_space=pl.ANY)
VMEM = pl.BlockSpec(memory_space=pltpu.VMEM)
SMEM = pl.BlockSpec(memory_space=pltpu.SMEM)


SWAP = [
    ((SEQS * a + r) * NY + b, (SEQS * b + r) * NY + a)
    for a in range(NY)
    for b in range(NY)
    for r in range(SEQS)
]


def around(size, shift):
    return [(i, (i + shift) % size) for i in range(size)]


def join_kernel(*refs):
    *parts, out = refs
    for part, (lo, hi) in zip(parts, COLS):
        out[:, lo:hi] = part[...].reshape(out.shape[0], hi - lo)


def join(rows, *arrays):
    return pl.pallas_call(
        join_kernel,
        out_shape=jax.ShapeDtypeStruct((rows, WIDTH), jnp.bfloat16),
        in_specs=[VMEM] * 4,
        out_specs=VMEM,
        compiler_params=pltpu.CompilerParams(vmem_limit_bytes=60 * MIB),
    )(*arrays)


NEAR = ((0, 2 * ROWS), (1, 2 * ROWS), (3, 2 * ROWS))
FAR = ((2, ROWS), (2, ROWS))


def gram_kernel(pieces, *refs):
    n = len(pieces)
    count = sum(rows for _, rows in pieces) // ROWS
    train, vals, rest = refs[0], refs[1 : n + 1], refs[n + 1 :]
    before, (mine, send, tbuf, vbuf, tsem, vsem) = rest[:-6], rest[-6:]
    x = lax.axis_index("x")
    first = lax.axis_index("core") == 0
    tcopy, vcopy, j = [], [], 0
    for i, (ref, (shift, rows)) in enumerate(zip(vals, pieces)):
        blocks = rows // ROWS
        vcopy.append(
            pltpu.make_async_copy(ref, vbuf.at[pl.ds(j * ROWS, rows)], vsem.at[i])
        )
        for h in range(blocks):
            b = 2 * lax.rem(x + shift, NX) + (h if blocks == 2 else i)
            tcopy.append(pltpu.make_async_copy(train.at[b], tbuf.at[j], tsem.at[j]))
            j += 1
    for c in (*vcopy, *tcopy):
        c.start()
    for c in vcopy:
        c.wait()
    for g, (lo, hi) in enumerate(COLS):
        acc = None
        for j in range(count):
            if g == 0:
                tcopy[j].wait()
            d = lax.dot_general(
                vbuf[j * ROWS : (j + 1) * ROWS, lo:hi],
                tbuf[j, :, lo:hi],
                (((1,), (1,)), ((), ())),
                preferred_element_type=jnp.float32,
            )
            acc = d if acc is None else acc + d
        keep = jnp.where(first, acc[:HALF], acc[HALF:])
        give = jnp.where(first, acc[HALF:], acc[:HALF])
        if before:
            keep, give = keep + before[0][g], give + before[1][g]
        mine[g] = keep
        send[g] = give


def grams(pieces, train, vals, before=()):
    half = jax.ShapeDtypeStruct((4, HALF, TOK), jnp.float32)
    count = sum(rows for _, rows in pieces) // ROWS
    return pl.pallas_call(
        functools.partial(gram_kernel, pieces),
        out_shape=(half, half),
        in_specs=[ANY] * (1 + len(pieces)) + [VMEM] * len(before),
        out_specs=(VMEM, VMEM),
        scratch_shapes=[
            pltpu.VMEM((count, TOK, WIDTH), jnp.bfloat16),
            pltpu.VMEM((count * ROWS, WIDTH), jnp.bfloat16),
            pltpu.SemaphoreType.DMA((count,)),
            pltpu.SemaphoreType.DMA((len(pieces),)),
        ],
        compiler_params=pltpu.CompilerParams(vmem_limit_bytes=GRAM_MIB * MIB),
        cost_estimate=pl.CostEstimate(
            flops=2 * count * ROWS * TOK * WIDTH,
            bytes_accessed=2 * count * (ROWS + TOK) * WIDTH,
            transcendentals=0,
        ),
    )(train, *vals, *before)


GRAM_MIB = 48


def score_kernel(tl, vl, mine, other, out):
    first = 3 * (2 * lax.axis_index("y") + lax.axis_index("core"))
    g = mine[...] + other[...]
    contrib = g[0] * g[2] + g[1] * g[3]
    places = lax.broadcasted_iota(jnp.int32, (VLEN, TOK), 0)
    tokens = lax.broadcasted_iota(jnp.int32, (1, TOK), 1)
    rows = lax.broadcasted_iota(jnp.int32, (4, 3), 0)
    cols = lax.broadcasted_iota(jnp.int32, (4, 3), 1)
    result = jnp.zeros((4, 3), jnp.float32)
    for s in range(3):
        block = contrib[s * VLEN : (s + 1) * VLEN]
        per_token = jnp.sum(
            jnp.where(places < vl[first + s], block, 0.0), axis=0, keepdims=True
        )
        start = jnp.int32(0)
        for k in range(4):
            end = start + tl[0, k]
            inside = (tokens >= start) & (tokens < end)
            total = jnp.sum(
                jnp.where(inside, per_token, 0.0), axis=1, keepdims=True
            )
            result = jnp.where((rows == k) & (cols == s), total, result)
            start = end
    out[...] = result * score_scale


def scores_of(tl, vl, mine, other):
    return pl.pallas_call(
        score_kernel,
        out_shape=jax.ShapeDtypeStruct((4, 3), jnp.float32),
        in_specs=[SMEM, SMEM, VMEM, VMEM],
        out_specs=VMEM,
        compiler_params=pltpu.CompilerParams(vmem_limit_bytes=16 * MIB),
    )(tl, vl, mine, other)


def local(tx, ta, tq, to, tl, vx, va, vq, vo, vl):
    val = join(VLEN, vx, va, vq, vo)
    val = lax.ppermute(val, ("x", "z", "y"), SWAP)
    tx, ta, tq, to, val = lax.optimization_barrier((tx, ta, tq, to, val))
    train = join(TOK, tx, ta, tq, to)
    full = lax.all_gather(train, "y", axis=0, tiled=False)
    own = lax.all_gather(val, "z", axis=0, tiled=True)
    right = lax.ppermute(own, "x", around(NX, -1))
    left = lax.ppermute(own, "x", around(NX, 1))
    far0 = lax.ppermute(left[:ROWS], "x", around(NX, 1))
    far1 = lax.ppermute(right[ROWS:], "x", around(NX, -1))
    near = grams(NEAR, full, (own, right, left))
    mine, send = grams(FAR, full, (far0, far1), near)
    other = lax.ppermute(send, "core", [(0, 1), (1, 0)])
    return scores_of(tl, vl, mine, other)


def solution(mesh):
    fine = Mesh(mesh.devices.reshape(NX, NZ, NY, NC), ("x", "z", "y", "core"))
    dp, fsdp = ("x", "z"), ("y", "core")
    in_specs = (
        (P(dp, fsdp),) * 4 + (P(dp, None),) + (P(dp, None, fsdp),) * 4 + (P(),)
    )
    return jax.shard_map(
        local, mesh=fine, in_specs=in_specs, out_specs=P(dp, fsdp), check_vma=False
    )
```

```python
import jax
import jax.numpy as jnp
from jax import lax
from jax.experimental import pallas as pl
from jax.experimental.pallas import tpu as pltpu
from jax.sharding import Mesh, PartitionSpec as P

score_scale = 0.015625

NX, NZ, NY, NC = 4, 12, 8, 2
TOK, VLEN = 256, 32
SEQS = 6
ROWS = SEQS * VLEN
HALF = ROWS // 2
COLS = ((0, 256), (256, 512), (512, 896), (896, 1152))
WIDTH = 1152
MIB = 1024 * 1024

ANY = pl.BlockSpec(memory_space=pl.ANY)
VMEM = pl.BlockSpec(memory_space=pltpu.VMEM)
SMEM = pl.BlockSpec(memory_space=pltpu.SMEM)


SWAP = [
    ((SEQS * a + r) * NY + b, (SEQS * b + r) * NY + a)
    for a in range(NY)
    for b in range(NY)
    for r in range(SEQS)
]


def around(size, shift):
    return [(i, (i + shift) % size) for i in range(size)]


def join_kernel(tx, ta, tq, to, vx, va, vq, vo, train, val):
    for t, v, (lo, hi) in zip((tx, ta, tq, to), (vx, va, vq, vo), COLS):
        train[:, lo:hi] = t[...]
        val[:, lo:hi] = v[0]


def join(*arrays):
    return pl.pallas_call(
        join_kernel,
        out_shape=(
            jax.ShapeDtypeStruct((TOK, WIDTH), jnp.bfloat16),
            jax.ShapeDtypeStruct((VLEN, WIDTH), jnp.bfloat16),
        ),
        in_specs=[VMEM] * 8,
        out_specs=(VMEM, VMEM),
        compiler_params=pltpu.CompilerParams(vmem_limit_bytes=60 * MIB),
    )(*arrays)


NEAR = (0, 1, 3)
PARAMS = dict(vmem_limit_bytes=48 * MIB)
PART = jax.ShapeDtypeStruct((4, HALF, TOK), jnp.float32)


def products(blocks, trains, waits=None):
    for g, (lo, hi) in enumerate(COLS):
        acc = None
        for j, (block, t) in enumerate(zip(blocks, trains)):
            if g == 0 and waits:
                waits[j].wait()
            d = lax.dot_general(
                block[:, lo:hi],
                t[:, lo:hi],
                (((1,), (1,)), ((), ())),
                preferred_element_type=jnp.float32,
            )
            acc = d if acc is None else acc + d
        yield g, acc[:HALF], acc[HALF:]


def near_kernel(train, *refs):
    vals, (mine, send, tfar, tbuf, vbuf, tsem, vsem) = refs[:3], refs[3:]
    x = lax.axis_index("x")
    first = lax.axis_index("core") == 0
    vcopy = [
        pltpu.make_async_copy(v, vbuf.at[i], vsem.at[i]) for i, v in enumerate(vals)
    ]
    tcopy = []
    for j in range(NY):
        shift = (*NEAR, 2)[j // 2]
        b = 2 * lax.rem(x + shift, NX) + j % 2
        target = tbuf.at[j] if j < 6 else tfar.at[j - 6]
        tcopy.append(pltpu.make_async_copy(train.at[b], target, tsem.at[j]))
    for c in (*vcopy, *tcopy):
        c.start()
    for c in vcopy:
        c.wait()
    blocks = [
        vbuf.at[j // 2, (j % 2) * ROWS : (j % 2 + 1) * ROWS] for j in range(6)
    ]
    for g, zero, one in products(blocks, [tbuf.at[j] for j in range(6)], tcopy):
        mine[g] = jnp.where(first, zero, one)
        send[g] = jnp.where(first, one, zero)
    for c in tcopy[6:]:
        c.wait()


def near_grams(train, *vals):
    return pl.pallas_call(
        near_kernel,
        out_shape=(PART, PART, jax.ShapeDtypeStruct((2, TOK, WIDTH), jnp.bfloat16)),
        in_specs=[ANY] * 4,
        out_specs=(VMEM,) * 3,
        scratch_shapes=[
            pltpu.VMEM((6, TOK, WIDTH), jnp.bfloat16),
            pltpu.VMEM((3, 2 * ROWS, WIDTH), jnp.bfloat16),
            pltpu.SemaphoreType.DMA((NY,)),
            pltpu.SemaphoreType.DMA((3,)),
        ],
        compiler_params=pltpu.CompilerParams(**PARAMS),
        cost_estimate=pl.CostEstimate(
            flops=12 * ROWS * TOK * WIDTH,
            bytes_accessed=12 * (ROWS + TOK) * WIDTH,
            transcendentals=0,
        ),
    )(train, *vals)


def far_kernel(tfar, far0, far1, mine0, send0, mine, send):
    first = lax.axis_index("core") == 0
    for g, zero, one in products([far0, far1], [tfar.at[0], tfar.at[1]]):
        mine[g] = mine0[g] + jnp.where(first, zero, one)
        send[g] = send0[g] + jnp.where(first, one, zero)


def far_grams(*arrays):
    return pl.pallas_call(
        far_kernel,
        out_shape=(PART, PART),
        in_specs=[VMEM] * 5,
        out_specs=(VMEM, VMEM),
        compiler_params=pltpu.CompilerParams(**PARAMS),
    )(*arrays)


def score_kernel(tl, vl, mine, other, out):
    first = 3 * (2 * lax.axis_index("y") + lax.axis_index("core"))
    g = mine[...] + other[...]
    contrib = g[0] * g[2] + g[1] * g[3]
    places = lax.broadcasted_iota(jnp.int32, (VLEN, TOK), 0)
    tokens = lax.broadcasted_iota(jnp.int32, (1, TOK), 1)
    rows = lax.broadcasted_iota(jnp.int32, (4, 3), 0)
    cols = lax.broadcasted_iota(jnp.int32, (4, 3), 1)
    result = jnp.zeros((4, 3), jnp.float32)
    for s in range(3):
        block = contrib[s * VLEN : (s + 1) * VLEN]
        per_token = jnp.sum(
            jnp.where(places < vl[first + s], block, 0.0), axis=0, keepdims=True
        )
        start = jnp.int32(0)
        for k in range(4):
            end = start + tl[0, k]
            inside = (tokens >= start) & (tokens < end)
            total = jnp.sum(
                jnp.where(inside, per_token, 0.0), axis=1, keepdims=True
            )
            result = jnp.where((rows == k) & (cols == s), total, result)
            start = end
    out[...] = result * score_scale


def scores_of(tl, vl, mine, other):
    return pl.pallas_call(
        score_kernel,
        out_shape=jax.ShapeDtypeStruct((4, 3), jnp.float32),
        in_specs=[SMEM, SMEM, VMEM, VMEM],
        out_specs=VMEM,
        compiler_params=pltpu.CompilerParams(vmem_limit_bytes=16 * MIB),
    )(tl, vl, mine, other)


def local(tx, ta, tq, to, tl, vx, va, vq, vo, vl):
    train, val = join(tx, ta, tq, to, vx, va, vq, vo)
    full = lax.all_gather(train, "y", axis=0, tiled=False)
    val = lax.ppermute(val, ("x", "z", "y"), SWAP)
    own = lax.all_gather(val, "z", axis=0, tiled=True)
    right = lax.ppermute(own, "x", around(NX, -1))
    left = lax.ppermute(own, "x", around(NX, 1))
    far0 = lax.ppermute(left[:ROWS], "x", around(NX, 1))
    far1 = lax.ppermute(right[ROWS:], "x", around(NX, -1))
    mine, send, tfar = near_grams(full, own, right, left)
    mine, send = far_grams(tfar, far0, far1, mine, send)
    other = lax.ppermute(send, "core", [(0, 1), (1, 0)])
    return scores_of(tl, vl, mine, other)


def solution(mesh):
    fine = Mesh(mesh.devices.reshape(NX, NZ, NY, NC), ("x", "z", "y", "core"))
    dp, fsdp = ("x", "z"), ("y", "core")
    in_specs = (
        (P(dp, fsdp),) * 4 + (P(dp, None),) + (P(dp, None, fsdp),) * 4 + (P(),)
    )
    return jax.shard_map(
        local, mesh=fine, in_specs=in_specs, out_specs=P(dp, fsdp), check_vma=False
    )
```

```python
import jax
import jax.numpy as jnp
from jax import lax
from jax.experimental import pallas as pl
from jax.experimental.pallas import tpu as pltpu
from jax.sharding import Mesh, PartitionSpec as P

score_scale = 0.015625

NX, NZ, NY, NC = 4, 12, 8, 2
TOK, VLEN = 256, 32
SEQS = 6
ROWS = SEQS * VLEN
HALF = ROWS // 2
COLS = ((0, 256), (256, 512), (512, 896), (896, 1152))
WIDTH = 1152
MIB = 1024 * 1024

ANY = pl.BlockSpec(memory_space=pl.ANY)
VMEM = pl.BlockSpec(memory_space=pltpu.VMEM)
SMEM = pl.BlockSpec(memory_space=pltpu.SMEM)


SWAP = [
    ((SEQS * a + r) * NY + b, (SEQS * b + r) * NY + a)
    for a in range(NY)
    for b in range(NY)
    for r in range(SEQS)
]


def around(size, shift):
    return [(i, (i + shift) % size) for i in range(size)]


def join_kernel(tx, ta, tq, to, vx, va, vq, vo, train, val, sems):
    copies = []
    for i, (t, v, (lo, hi)) in enumerate(zip((tx, ta, tq, to), (vx, va, vq, vo), COLS)):
        copies.append(pltpu.make_async_copy(t, train.at[:, lo:hi], sems.at[2 * i]))
        copies.append(pltpu.make_async_copy(v.at[0], val.at[:, lo:hi], sems.at[2 * i + 1]))
    for c in copies:
        c.start()
    for c in copies:
        c.wait()


def join(*arrays):
    return pl.pallas_call(
        join_kernel,
        out_shape=(
            jax.ShapeDtypeStruct((TOK, WIDTH), jnp.bfloat16),
            jax.ShapeDtypeStruct((VLEN, WIDTH), jnp.bfloat16),
        ),
        in_specs=[ANY] * 8,
        out_specs=(VMEM, VMEM),
        scratch_shapes=[pltpu.SemaphoreType.DMA((8,))],
        compiler_params=pltpu.CompilerParams(vmem_limit_bytes=60 * MIB),
    )(*arrays)


NEAR = (0, 1, 3)
PARAMS = dict(vmem_limit_bytes=48 * MIB)
PART = jax.ShapeDtypeStruct((4, HALF, TOK), jnp.float32)


def products(blocks, trains, waits=None):
    for g, (lo, hi) in enumerate(COLS):
        acc = None
        for j, (block, t) in enumerate(zip(blocks, trains)):
            if g == 0 and waits:
                waits[j].wait()
            d = lax.dot_general(
                block[:, lo:hi],
                t[:, lo:hi],
                (((1,), (1,)), ((), ())),
                preferred_element_type=jnp.float32,
            )
            acc = d if acc is None else acc + d
        yield g, acc[:HALF], acc[HALF:]


def near_kernel(train, *refs):
    vals, (mine, send, tfar, tbuf, vbuf, tsem, vsem) = refs[:3], refs[3:]
    x = lax.axis_index("x")
    first = lax.axis_index("core") == 0
    vcopy = [
        pltpu.make_async_copy(v, vbuf.at[i], vsem.at[i]) for i, v in enumerate(vals)
    ]
    tcopy = []
    for j in range(NY):
        shift = (*NEAR, 2)[j // 2]
        b = 2 * lax.rem(x + shift, NX) + j % 2
        target = tbuf.at[j] if j < 6 else tfar.at[j - 6]
        tcopy.append(pltpu.make_async_copy(train.at[b], target, tsem.at[j]))
    for c in (*vcopy, *tcopy):
        c.start()
    for c in vcopy:
        c.wait()
    blocks = [
        vbuf.at[j // 2, (j % 2) * ROWS : (j % 2 + 1) * ROWS] for j in range(6)
    ]
    for g, zero, one in products(blocks, [tbuf.at[j] for j in range(6)], tcopy):
        mine[g] = jnp.where(first, zero, one)
        send[g] = jnp.where(first, one, zero)
    for c in tcopy[6:]:
        c.wait()


def near_grams(train, *vals):
    return pl.pallas_call(
        near_kernel,
        out_shape=(PART, PART, jax.ShapeDtypeStruct((2, TOK, WIDTH), jnp.bfloat16)),
        in_specs=[ANY] * 4,
        out_specs=(VMEM,) * 3,
        scratch_shapes=[
            pltpu.VMEM((6, TOK, WIDTH), jnp.bfloat16),
            pltpu.VMEM((3, 2 * ROWS, WIDTH), jnp.bfloat16),
            pltpu.SemaphoreType.DMA((NY,)),
            pltpu.SemaphoreType.DMA((3,)),
        ],
        compiler_params=pltpu.CompilerParams(**PARAMS),
        cost_estimate=pl.CostEstimate(
            flops=12 * ROWS * TOK * WIDTH,
            bytes_accessed=12 * (ROWS + TOK) * WIDTH,
            transcendentals=0,
        ),
    )(train, *vals)


def far_kernel(tfar, far0, far1, mine0, send0, mine, send):
    first = lax.axis_index("core") == 0
    for g, zero, one in products([far0, far1], [tfar.at[0], tfar.at[1]]):
        mine[g] = mine0[g] + jnp.where(first, zero, one)
        send[g] = send0[g] + jnp.where(first, one, zero)


def far_grams(*arrays):
    return pl.pallas_call(
        far_kernel,
        out_shape=(PART, PART),
        in_specs=[VMEM] * 5,
        out_specs=(VMEM, VMEM),
        compiler_params=pltpu.CompilerParams(**PARAMS),
    )(*arrays)


def score_kernel(tl, vl, mine, other, out):
    first = 3 * (2 * lax.axis_index("y") + lax.axis_index("core"))
    g = mine[...] + other[...]
    contrib = g[0] * g[2] + g[1] * g[3]
    places = lax.broadcasted_iota(jnp.int32, (VLEN, TOK), 0)
    tokens = lax.broadcasted_iota(jnp.int32, (1, TOK), 1)
    rows = lax.broadcasted_iota(jnp.int32, (4, 3), 0)
    cols = lax.broadcasted_iota(jnp.int32, (4, 3), 1)
    result = jnp.zeros((4, 3), jnp.float32)
    for s in range(3):
        block = contrib[s * VLEN : (s + 1) * VLEN]
        per_token = jnp.sum(
            jnp.where(places < vl[first + s], block, 0.0), axis=0, keepdims=True
        )
        start = jnp.int32(0)
        for k in range(4):
            end = start + tl[0, k]
            inside = (tokens >= start) & (tokens < end)
            total = jnp.sum(
                jnp.where(inside, per_token, 0.0), axis=1, keepdims=True
            )
            result = jnp.where((rows == k) & (cols == s), total, result)
            start = end
    out[...] = result * score_scale


def scores_of(tl, vl, mine, other):
    return pl.pallas_call(
        score_kernel,
        out_shape=jax.ShapeDtypeStruct((4, 3), jnp.float32),
        in_specs=[SMEM, SMEM, VMEM, VMEM],
        out_specs=VMEM,
        compiler_params=pltpu.CompilerParams(vmem_limit_bytes=16 * MIB),
    )(tl, vl, mine, other)


def local(tx, ta, tq, to, tl, vx, va, vq, vo, vl):
    train, val = join(tx, ta, tq, to, vx, va, vq, vo)
    full = lax.all_gather(train, "y", axis=0, tiled=False)
    val = lax.ppermute(val, ("x", "z", "y"), SWAP)
    own = lax.all_gather(val, "z", axis=0, tiled=True)
    right = lax.ppermute(own, "x", around(NX, -1))
    left = lax.ppermute(own, "x", around(NX, 1))
    far0 = lax.ppermute(left[:ROWS], "x", around(NX, 1))
    far1 = lax.ppermute(right[ROWS:], "x", around(NX, -1))
    mine, send, tfar = near_grams(full, own, right, left)
    mine, send = far_grams(tfar, far0, far1, mine, send)
    other = lax.ppermute(send, "core", [(0, 1), (1, 0)])
    return scores_of(tl, vl, mine, other)


def solution(mesh):
    fine = Mesh(mesh.devices.reshape(NX, NZ, NY, NC), ("x", "z", "y", "core"))
    dp, fsdp = ("x", "z"), ("y", "core")
    in_specs = (
        (P(dp, fsdp),) * 4 + (P(dp, None),) + (P(dp, None, fsdp),) * 4 + (P(),)
    )
    return jax.shard_map(
        local, mesh=fine, in_specs=in_specs, out_specs=P(dp, fsdp), check_vma=False
    )
```
